256 devices in a mesh: dp: 32 (over y, x, core), tensor: 8 (over z).
Axes of the slice: x: 4, y: 4, z: 8, core: 2. Of those that a mesh axis runs over, the one named last changes fastest.
Arguments:
- input_token_rows: bfloat16 [16384, 28672], P('dp', 'tensor'), may hold values from -120 to 120
- output_gradient_rows: bfloat16 [16384, 8192], P('dp'), may hold values from -1000 to 1000
- frozen_base_matrix: bfloat16 [8192, 28672], P('dp', 'tensor'), may hold values from -6 to 6
- left_lowrank_factor: float32 [256, 28672], P('dp', 'tensor'), may hold values from -6 to 6
- left_first_moment: float32 [256, 28672], P('dp', 'tensor'), may hold values from -4.5776367e-05 to 4.5776367e-05
- left_second_moment: float32 [256, 28672], P('dp', 'tensor'), may hold values from 5e-11 to 5e-10
- right_lowrank_factor: float32 [8192, 256], P('dp'), may hold values from -32 to 32
- right_first_moment: float32 [8192, 256], P('dp'), may hold values from -9.1552734e-05 to 9.1552734e-05
- right_second_moment: float32 [8192, 256], P('dp'), may hold values from 2e-10 to 2e-09
Outputs:
- merged_weight: bfloat16 [8192, 28672], P('dp', 'tensor')
The draws below stay inside these ranges and needn't reach their ends.
All inputs are finite; a program needn't handle non-finite values.
Results may differ from the reference program's by a relative error of at most 0.001.
The reference program's roundings to bfloat16 on the way count: a program that leaves them out, or rounds other values in their place, can miss the bound.
Values may be sent and summed in bfloat16 or wider, within the bound.
No kernel may reach another device: no remote copies, remote signals or barrier semaphores. Data moves between devices by JAX's collectives and lax.ppermute only.
A program may use at most 128 MiB of HBM per device.

```python
import math
import jax
import jax.numpy as jnp
from jax import lax

MODEL_WIDTH = 8192
HIDDEN_UNITS = 28672
FACTOR_RANK = 256
STEP = 5000
TOKENS = 16384
N_DP = 32


def spread_scales(key, shape, top):
    return jnp.exp(jax.random.uniform(key, shape, jnp.float32) * math.log(top))


def scaled_field(key, rows, columns, row_top, trend_power):
    keys = jax.random.split(key, 3)
    noise = jnp.clip(jax.random.normal(keys[0], (rows, columns), jnp.float32), -6.0, 6.0)
    trend = jnp.power(3.0, trend_power * jnp.arange(columns, dtype=jnp.float32) / columns)
    column_scale = spread_scales(keys[1], (1, columns), 10.0) * trend
    row_scale = spread_scales(keys[2], (rows, 1), row_top)
    return noise * row_scale * column_scale / 20.0


def draw_input_token_rows(key, part):
    key = jax.random.fold_in(key, 7)
    field = scaled_field(key, TOKENS, HIDDEN_UNITS, 10.0, 0.5)
    return field.astype(jnp.bfloat16)


def draw_output_gradient_rows(key, part):
    key = jax.random.fold_in(key, 13)
    field = scaled_field(key, TOKENS, MODEL_WIDTH, 10.0, 2.0)
    return field.astype(jnp.bfloat16)


def rising_factor(key):
    noise = jnp.clip(jax.random.normal(key, (MODEL_WIDTH, FACTOR_RANK), jnp.float32), -6.0, 6.0)
    trend = jnp.power(3.0, jnp.arange(FACTOR_RANK, dtype=jnp.float32) / FACTOR_RANK)
    return noise * trend[None, :]


def draw_right_lowrank_factor(key, part):
    key = jax.random.fold_in(key, 19)
    field = rising_factor(key)
    return field.astype(jnp.float32)


def level_of(key, dims, cuts, smallest, high):
    gain, own = 1.0, jax.random.fold_in(key, 6)
    for axis_at, blocks in cuts:
        draws = jnp.exp(jax.random.uniform(jax.random.fold_in(own, axis_at), (blocks,), jnp.float32, smallest / len(cuts), high / len(cuts)))
        gain = gain * jnp.repeat(draws, dims[axis_at] // blocks).reshape([-1 if axis == axis_at else 1 for axis in range(len(dims))])
    return gain


def normal_values(rng, dims, deviation, most, pieces=(), kind=jnp.bfloat16):
    drawn = deviation * jax.random.normal(rng, dims, jnp.float32)
    if pieces:
        drawn = drawn * level_of(rng, dims, pieces, -0.22, 0.18)
    return jnp.clip(drawn, -most, most).astype(kind)


def setup_inputs(seed: int = 0) -> dict:
    splits = jax.random.split(jax.random.key(seed), 10)
    return {
        "input_token_rows": draw_input_token_rows(jax.random.fold_in(splits[9], 71), 0),
        "output_gradient_rows": draw_output_gradient_rows(jax.random.fold_in(splits[9], 71), 0),
        "frozen_base_matrix": normal_values(splits[2], (MODEL_WIDTH, HIDDEN_UNITS), 1.0, 6.0, ((0, 32), (1, 8))),
        "left_lowrank_factor": normal_values(splits[3], (FACTOR_RANK, HIDDEN_UNITS), 1.0, 6.0, ((0, 32), (1, 8)), jnp.float32),
        "left_first_moment": normal_values(splits[4], (FACTOR_RANK, HIDDEN_UNITS), 0.000008, 4.57763671875e-05, ((0, 32), (1, 8)), jnp.float32),
        "left_second_moment": jnp.clip(jnp.exp(math.log(4.999999858590343e-10) - 2.3025851 * jax.random.uniform(splits[5], (FACTOR_RANK, HIDDEN_UNITS), jnp.float32) ** level_of(splits[5], (FACTOR_RANK, HIDDEN_UNITS), ((0, 32), (1, 8)), -0.2, 0.2)), 5.00000006675716e-11, 4.999999858590343e-10),
        "right_lowrank_factor": draw_right_lowrank_factor(jax.random.fold_in(splits[9], 71), 0),
        "right_first_moment": normal_values(splits[7], (MODEL_WIDTH, FACTOR_RANK), 0.000015, 9.1552734375e-05, ((0, 32),), jnp.float32),
        "right_second_moment": jnp.clip(jnp.exp(math.log(1.999999943436137e-09) - 2.3025851 * jax.random.uniform(splits[8], (MODEL_WIDTH, FACTOR_RANK), jnp.float32) ** level_of(splits[8], (MODEL_WIDTH, FACTOR_RANK), ((0, 32),), -0.2, 0.2)), 2.000000026702864e-10, 1.999999943436137e-09),
    }


first_decay = 0.9
second_decay = 0.999
adam_epsilon = 1e-08
learn_rate = 0.05
clip_limit = 1.0
norm_epsilon = 1e-06

def moment_update_step(param, first, second, grad):
    first_new = first_decay * first + (1.0 - first_decay) * grad
    second_new = second_decay * second + (1.0 - second_decay) * grad * grad
    first_fix = 1.0 - first_decay ** STEP
    second_fix = 1.0 - second_decay ** STEP
    return param - learn_rate * (first_new / first_fix) / (jnp.sqrt(second_new / second_fix) + adam_epsilon)

def reference(input_token_rows, output_gradient_rows, frozen_base_matrix, left_lowrank_factor, left_first_moment, left_second_moment, right_lowrank_factor, right_first_moment, right_second_moment):
    hidden_scale = 1.0 / math.sqrt(HIDDEN_UNITS)
    rank_scale = 1.0 / math.sqrt(FACTOR_RANK)
    left_factor_half = left_lowrank_factor.astype(jnp.bfloat16)
    right_factor_half = right_lowrank_factor.astype(jnp.bfloat16)
    act = jnp.dot(input_token_rows, left_factor_half.T, preferred_element_type=jnp.float32) * hidden_scale
    act_bf = act.astype(jnp.bfloat16)
    back = jnp.dot(output_gradient_rows, right_factor_half, preferred_element_type=jnp.float32) * rank_scale
    back_bf = back.astype(jnp.bfloat16)
    left_factor_gradient = jnp.dot(back_bf.T, input_token_rows, preferred_element_type=jnp.float32) * hidden_scale
    right_factor_gradient = jnp.dot(output_gradient_rows.T, act_bf, preferred_element_type=jnp.float32) * rank_scale
    squares = jnp.sum(left_factor_gradient * left_factor_gradient) + jnp.sum(right_factor_gradient * right_factor_gradient)
    gradient_clipper = jnp.minimum(1.0, clip_limit / (jnp.sqrt(squares) + norm_epsilon))
    updated_left_factor = moment_update_step(left_lowrank_factor, left_first_moment, left_second_moment, gradient_clipper * left_factor_gradient)
    updated_right_factor = moment_update_step(right_lowrank_factor, right_first_moment, right_second_moment, gradient_clipper * right_factor_gradient)
    new_a_bf = updated_left_factor.astype(jnp.bfloat16)
    new_b_bf = updated_right_factor.astype(jnp.bfloat16)
    weight_blocks = frozen_base_matrix.reshape(N_DP, MODEL_WIDTH // N_DP, HIDDEN_UNITS)
    factor_blocks = new_b_bf.reshape(N_DP, MODEL_WIDTH // N_DP, FACTOR_RANK)

    def merge_block(pair):
        weight_rows, factor_rows = pair
        product = jnp.dot(factor_rows, new_a_bf, preferred_element_type=jnp.float32)
        return (weight_rows.astype(jnp.float32) + product * rank_scale).astype(jnp.bfloat16)
    merged = lax.map(merge_block, (weight_blocks, factor_blocks))
    return merged.reshape(MODEL_WIDTH, HIDDEN_UNITS)
```

```python
import math

import jax
import jax.numpy as jnp
import numpy as np
from jax import lax
from jax.sharding import Mesh
from jax.sharding import PartitionSpec as P

HIDDEN_UNITS = 28672
FACTOR_RANK = 256
STEP = 5000

first_decay = 0.9
second_decay = 0.999
adam_epsilon = 1e-08
learn_rate = 0.05
clip_limit = 1.0
norm_epsilon = 1e-06

bf16 = jnp.bfloat16
f32 = jnp.float32
DP = ("y", "x", "core")


def moment_update_step(param, first, second, grad):
    first_new = first_decay * first + (1.0 - first_decay) * grad
    second_new = second_decay * second + (1.0 - second_decay) * grad * grad
    first_fix = 1.0 - first_decay**STEP
    second_fix = 1.0 - second_decay**STEP
    return param - learn_rate * (first_new / first_fix) / (
        jnp.sqrt(second_new / second_fix) + adam_epsilon
    )


def dp_index(y, x, c):
    return (y * 4 + x) * 2 + c


def plane_pairs(first, k):
    pairs = []
    for y in range(4):
        for x in range(4):
            for c in range(2):
                if (c == 0) == first:
                    target = dp_index(y, (x + k) % 4, c)
                else:
                    target = dp_index((y + k) % 4, x, c)
                pairs.append((dp_index(y, x, c), target))
    return pairs


def shift_p(v, k):
    return lax.ppermute(v, DP, plane_pairs(True, k))


def shift_q(v, k):
    return lax.ppermute(v, DP, plane_pairs(False, k))


def swap_core(v):
    return lax.ppermute(v, "core", [(0, 1), (1, 0)])


def shift_z(v, k):
    return lax.ppermute(v, "z", [(i, (i + k) % 8) for i in range(8)])


def flip(v, axis, n, bit):
    return lax.ppermute(v, axis, [(i, i ^ bit) for i in range(n)])


def pick(stack, index):
    return lax.dynamic_index_in_dim(stack, index, 0, keepdims=False)


def gather_plane(block, p, q, core):
    got = [block] + [shift_p(block, k) for k in range(1, 4)]
    got = jnp.stack(got)
    ordered = jnp.stack([pick(got, (p - j) % 4) for j in range(4)])
    rows = [ordered] + [shift_q(ordered, k) for k in range(1, 4)]
    rows = jnp.stack(rows)
    mine = jnp.stack([pick(rows, (q - j) % 4) for j in range(4)])
    other = swap_core(mine)
    zero = jnp.where(core == 0, mine, other)
    one = jnp.where(core == 0, other, mine)
    return jnp.stack([zero, one.swapaxes(0, 1)], axis=2)


def scatter_plane(terms, p, q, core):
    zero = terms[:, :, 0].swapaxes(0, 1)
    one = terms[:, :, 1]
    keep = jnp.where(core == 0, zero, one)
    send = jnp.where(core == 0, one, zero)
    total = keep + swap_core(send)
    parts = [pick(total, (p + k) % 4) for k in range(4)]
    total = parts[0]
    for k in range(1, 4):
        total = total + shift_p(parts[k], k)
    parts = [pick(total, (q + k) % 4) for k in range(4)]
    total = parts[0]
    for k in range(1, 4):
        total = total + shift_q(parts[k], k)
    return total


def local(
    input_token_rows,
    output_gradient_rows,
    frozen_base_matrix,
    left_lowrank_factor,
    left_first_moment,
    left_second_moment,
    right_lowrank_factor,
    right_first_moment,
    right_second_moment,
):
    hidden_scale = 1.0 / math.sqrt(HIDDEN_UNITS)
    rank_scale = 1.0 / math.sqrt(FACTOR_RANK)
    y, x, core, z = (lax.axis_index(n) for n in ("y", "x", "core", "z"))
    p = jnp.where(core == 0, x, y)
    q = jnp.where(core == 0, y, x)

    right_t = right_lowrank_factor.T
    b_part = lax.dynamic_slice_in_dim(right_t, (z % 4) * 64, 64, 0).astype(bf16)
    b_rows = gather_plane(b_part, p, q, core)
    b_rows = b_rows.reshape(32, 64, 256).swapaxes(0, 1).reshape(64, 8192)
    back_part = (
        lax.dot_general(
            b_rows, output_gradient_rows, (((1,), (1,)), ((), ())), preferred_element_type=f32
        )
        * rank_scale
    ).astype(bf16)
    backs = jnp.stack(
        [back_part, shift_z(back_part, 1), shift_z(back_part, 2), shift_z(back_part, -1)]
    )
    back = jnp.concatenate([pick(backs, (z - j) % 4) for j in range(4)], axis=0)
    a_term = jnp.dot(back, input_token_rows, preferred_element_type=f32)
    grad_a = scatter_plane(a_term.reshape(4, 4, 2, 8, 3584), p, q, core) * hidden_scale

    a_rows = gather_plane(left_lowrank_factor.astype(bf16), p, q, core).reshape(256, 3584)
    act_part = lax.dot_general(
        a_rows, input_token_rows, (((1,), (1,)), ((), ())), preferred_element_type=f32
    ).reshape(8, 32, 512)
    act = pick(act_part, z)
    for k in range(1, 8):
        act = act + shift_z(pick(act_part, (z + k) % 8), k)
    act = (act * hidden_scale).astype(bf16)
    b_term = jnp.dot(act, output_gradient_rows, preferred_element_type=f32)
    b_term = b_term.reshape(32, 4, 4, 2, 256).transpose(1, 2, 3, 0, 4)
    grad_b = scatter_plane(b_term, p, q, core) * rank_scale

    squares = jnp.sum(grad_a * grad_a) + jnp.sum(grad_b * grad_b)
    squares = jnp.broadcast_to(squares, (8, 128))
    squares = squares + swap_core(squares)
    for axis, n, bit in (
        ("x", 4, 1),
        ("x", 4, 2),
        ("y", 4, 1),
        ("y", 4, 2),
        ("z", 8, 1),
        ("z", 8, 2),
        ("z", 8, 4),
    ):
        squares = squares + flip(squares, axis, n, bit)
    clipper = jnp.minimum(1.0, clip_limit / (jnp.sqrt(squares[0, 0]) + norm_epsilon))

    new_a = moment_update_step(
        left_lowrank_factor, left_first_moment, left_second_moment, clipper * grad_a
    ).astype(bf16)

    def own_ranks(v):
        return lax.dynamic_slice_in_dim(v.T, z * 32, 32, 0)

    new_b = moment_update_step(
        own_ranks(right_lowrank_factor),
        own_ranks(right_first_moment),
        own_ranks(right_second_moment),
        clipper * grad_b,
    ).astype(bf16)
    for bit in (1, 2, 4):
        other = flip(new_b, "z", 8, bit)
        low = (z & bit) == 0
        new_b = jnp.concatenate(
            [jnp.where(low, new_b, other), jnp.where(low, other, new_b)], axis=0
        )
    new_a = gather_plane(new_a, p, q, core).reshape(256, 3584)
    product = lax.dot_general(new_b, new_a, (((0,), (0,)), ((), ())), preferred_element_type=f32)
    return (frozen_base_matrix.astype(f32) + product * rank_scale).astype(bf16)


def solution(mesh):
    grid = Mesh(np.asarray(mesh.devices).reshape(4, 4, 2, 8), ("y", "x", "core", "z"))
    split = P(DP, "z")
    rows = P(DP, None)
    return jax.shard_map(
        local,
        mesh=grid,
        in_specs=(split, rows, split, split, split, split, rows, rows, rows),
        out_specs=split,
        check_vma=False,
    )
```

```python
import math

import jax
import jax.numpy as jnp
import numpy as np
from jax import lax
from jax.sharding import Mesh
from jax.sharding import PartitionSpec as P

HIDDEN_UNITS = 28672
FACTOR_RANK = 256
STEP = 5000

first_decay = 0.9
second_decay = 0.999
adam_epsilon = 1e-08
learn_rate = 0.05
clip_limit = 1.0
norm_epsilon = 1e-06

bf16 = jnp.bfloat16
f32 = jnp.float32
DP = ("y", "x", "core")


def moment_update_step(param, first, second, grad):
    first_new = first_decay * first + (1.0 - first_decay) * grad
    second_new = second_decay * second + (1.0 - second_decay) * grad * grad
    first_fix = 1.0 - first_decay**STEP
    second_fix = 1.0 - second_decay**STEP
    return param - learn_rate * (first_new / first_fix) / (
        jnp.sqrt(second_new / second_fix) + adam_epsilon
    )


def dp_index(y, x, c):
    return (y * 4 + x) * 2 + c


def plane_pairs(first, k):
    pairs = []
    for y in range(4):
        for x in range(4):
            for c in range(2):
                if (c == 0) == first:
                    target = dp_index(y, (x + k) % 4, c)
                else:
                    target = dp_index((y + k) % 4, x, c)
                pairs.append((dp_index(y, x, c), target))
    return pairs


def shift_p(v, k):
    return lax.ppermute(v, DP, plane_pairs(True, k))


def shift_q(v, k):
    return lax.ppermute(v, DP, plane_pairs(False, k))


def swap_core(v):
    return lax.ppermute(v, "core", [(0, 1), (1, 0)])


def shift_z(v, k):
    return lax.ppermute(v, "z", [(i, (i + k) % 8) for i in range(8)])


def flip(v, axis, n, bit):
    return lax.ppermute(v, axis, [(i, i ^ bit) for i in range(n)])


def pick(stack, index):
    return lax.dynamic_index_in_dim(stack, index, 0, keepdims=False)


def tiles(v):
    rows, columns = v.shape
    return v.reshape(rows // 8, 8, columns // 128, 128).swapaxes(1, 2).reshape(-1, 128)


def untile(v, rows, columns):
    count = v.shape[0]
    v = v.reshape(count, rows // 8, columns // 128, 8, 128).swapaxes(2, 3)
    return v.reshape(count, rows, columns)


def by_offset(stack, index):
    return jnp.stack([pick(stack, (index - j) % 4) for j in range(4)])


def join_cores(mine, other, core):
    zero = jnp.where(core == 0, mine, other)
    one = jnp.where(core == 0, other, mine)
    return jnp.stack([zero, one.swapaxes(0, 1)], axis=2)


def local(
    input_token_rows,
    output_gradient_rows,
    frozen_base_matrix,
    left_lowrank_factor,
    left_first_moment,
    left_second_moment,
    right_lowrank_factor,
    right_first_moment,
    right_second_moment,
):
    hidden_scale = 1.0 / math.sqrt(HIDDEN_UNITS)
    rank_scale = 1.0 / math.sqrt(FACTOR_RANK)
    y, x, core, z = (lax.axis_index(n) for n in ("y", "x", "core", "z"))
    p = jnp.where(core == 0, x, y)
    q = jnp.where(core == 0, y, x)

    b_block = lax.dynamic_slice_in_dim(right_lowrank_factor, (z % 2) * 128, 128, 1)
    block = jnp.concatenate([tiles(left_lowrank_factor), b_block], axis=0).astype(bf16)
    stack = jnp.stack([block] + [shift_p(block, k) for k in (1, 2, 3)])
    stack = by_offset(stack, p)
    stack = jnp.stack([stack] + [shift_q(stack, k) for k in (1, 2, 3)])
    stack = by_offset(stack, q)
    blocks = join_cores(stack, swap_core(stack), core).reshape(32, 480, 128)
    a_rows = untile(blocks[:, :224], 8, 3584).reshape(256, 3584)
    b_rows = blocks[:, 224:].reshape(8192, 128)

    act_part = lax.dot_general(
        a_rows, input_token_rows, (((1,), (1,)), ((), ())), preferred_element_type=f32
    ).reshape(4, 2, 32, 512)
    act_send = lax.dynamic_index_in_dim(act_part, 1 - z % 2, 1, keepdims=False)
    act_keep = lax.dynamic_index_in_dim(act_part, z % 2, 1, keepdims=False)
    b_rows, act_send = lax.optimization_barrier((b_rows, act_send))
    act_got = flip(act_send, "z", 8, 1)
    back_part = (
        lax.dot_general(
            b_rows, output_gradient_rows, (((0,), (1,)), ((), ())), preferred_element_type=f32
        )
        * rank_scale
    ).astype(bf16)
    back_other = flip(back_part, "z", 8, 1)
    act_got, back_other = lax.optimization_barrier((act_got, back_other))
    act_pair = act_keep + act_got
    act_pieces = [pick(act_pair, (z // 2 + k) % 4) for k in range(4)]
    low = z % 2 == 0
    back = jnp.concatenate(
        [jnp.where(low, back_part, back_other), jnp.where(low, back_other, back_part)], axis=0
    )
    back, act_pieces = lax.optimization_barrier((back, act_pieces))
    a_term = jnp.dot(back, input_token_rows, preferred_element_type=f32)
    act = act_pieces[0]
    for k in range(1, 4):
        act = act + shift_z(act_pieces[k], 2 * k)
    act = (act * hidden_scale).astype(bf16)
    b_term = jnp.dot(act, output_gradient_rows, preferred_element_type=f32)

    a_term = a_term.reshape(4, 4, 2, 8, 28, 128).swapaxes(3, 4).reshape(4, 4, 2, 224, 128)
    b_term = b_term.reshape(4, 8, 4, 4, 2, 2, 128).transpose(2, 3, 4, 0, 5, 1, 6)
    b_term = b_term.reshape(4, 4, 2, 64, 128)
    halves = []
    for term in (a_term, b_term):
        zero = term[:, :, 0].swapaxes(0, 1)
        one = term[:, :, 1]
        keep = jnp.where(core == 0, zero, one)
        got = swap_core(jnp.where(core == 0, one, zero))
        halves.append((keep, got))
    parts = []
    for k in range(4):
        parts.append(
            jnp.concatenate(
                [pick(keep, (p + k) % 4) + pick(got, (p + k) % 4) for keep, got in halves], axis=1
            )
        )
    total = parts[0]
    for k in range(1, 4):
        total = total + shift_p(parts[k], k)
    parts = [pick(total, (q + k) % 4) for k in range(4)]
    total = parts[0]
    for k in range(1, 4):
        total = total + shift_q(parts[k], k)
    grad_a = total[:224] * hidden_scale
    grad_b = total[224:] * rank_scale

    squares = jnp.sum(grad_a * grad_a, axis=0) + jnp.sum(grad_b * grad_b, axis=0)
    squares = lax.all_to_all(
        jnp.broadcast_to(squares, (256, 128)), ("y", "x", "core", "z"), 0, 0, tiled=True
    )
    other = flip(grad_b, "z", 8, 1)
    squares, other = lax.optimization_barrier((squares, other))
    pair = jnp.concatenate([jnp.where(low, grad_b, other), jnp.where(low, other, grad_b)], axis=0)
    clipper = jnp.minimum(1.0, clip_limit / (jnp.sqrt(jnp.sum(squares)) + norm_epsilon))

    new_a = moment_update_step(
        tiles(left_lowrank_factor),
        tiles(left_first_moment),
        tiles(left_second_moment),
        clipper * grad_a,
    ).astype(bf16)
    copies = jnp.broadcast_to(new_a, (16, 224, 128))
    copies, pair = lax.optimization_barrier((copies, pair))
    mine = lax.all_to_all(copies, ("y", "x"), 0, 0, tiled=True)
    pairs = [pair] + [shift_z(pair, 2 * k) for k in range(1, 4)]
    mine, pairs = lax.optimization_barrier((mine, pairs))
    other = swap_core(mine)
    whole_grad_b = by_offset(jnp.stack(pairs), z // 2).reshape(8, 64, 128)
    whole_grad_b = untile(whole_grad_b, 32, 256).reshape(256, 256)
    new_b = moment_update_step(
        right_lowrank_factor.T, right_first_moment.T, right_second_moment.T, clipper * whole_grad_b
    ).astype(bf16)
    fresh = jnp.stack([jnp.where(core == 0, mine, other), jnp.where(core == 0, other, mine)], axis=1)
    new_a = untile(fresh.reshape(32, 224, 128), 8, 3584).reshape(256, 3584)
    product = lax.dot_general(new_b, new_a, (((0,), (0,)), ((), ())), preferred_element_type=f32)
    return (frozen_base_matrix.astype(f32) + product * rank_scale).astype(bf16)


def solution(mesh):
    grid = Mesh(np.asarray(mesh.devices).reshape(4, 4, 2, 8), ("y", "x", "core", "z"))
    split = P(DP, "z")
    rows = P(DP, None)
    return jax.shard_map(
        local,
        mesh=grid,
        in_specs=(split, rows, split, split, split, split, rows, rows, rows),
        out_specs=split,
        check_vma=False,
    )
```

```python
import math

import jax
import jax.numpy as jnp
import numpy as np
from jax import lax
from jax.sharding import Mesh
from jax.sharding import PartitionSpec as P

HIDDEN_UNITS = 28672
FACTOR_RANK = 256
STEP = 5000

first_decay = 0.9
second_decay = 0.999
adam_epsilon = 1e-08
learn_rate = 0.05
clip_limit = 1.0
norm_epsilon = 1e-06

bf16 = jnp.bfloat16
f32 = jnp.float32
DP = ("y", "x", "core")


def moment_update_step(param, first, second, grad):
    first_new = first_decay * first + (1.0 - first_decay) * grad
    second_new = second_decay * second + (1.0 - second_decay) * grad * grad
    first_fix = 1.0 - first_decay**STEP
    second_fix = 1.0 - second_decay**STEP
    return param - learn_rate * (first_new / first_fix) / (
        jnp.sqrt(second_new / second_fix) + adam_epsilon
    )


def dp_index(y, x, c):
    return (y * 4 + x) * 2 + c


def plane_pairs(first, k):
    pairs = []
    for y in range(4):
        for x in range(4):
            for c in range(2):
                if (c == 0) == first:
                    target = dp_index(y, (x + k) % 4, c)
                else:
                    target = dp_index((y + k) % 4, x, c)
                pairs.append((dp_index(y, x, c), target))
    return pairs


def shift_p(v, k):
    return lax.ppermute(v, DP, plane_pairs(True, k))


def shift_q(v, k):
    return lax.ppermute(v, DP, plane_pairs(False, k))


def swap_core(v):
    return lax.ppermute(v, "core", [(0, 1), (1, 0)])


def shift_z(v, k):
    return lax.ppermute(v, "z", [(i, (i + k) % 8) for i in range(8)])


def flip(v, axis, n, bit):
    return lax.ppermute(v, axis, [(i, i ^ bit) for i in range(n)])


def swap_pairs(v):
    return lax.ppermute(v, "z", [(i, (i + 1) % 8 if i % 2 else (i - 1) % 8) for i in range(8)])


def pick(stack, index):
    return lax.dynamic_index_in_dim(stack, index, 0, keepdims=False)


def ahead(stack, index):
    return jnp.stack([pick(stack, (index + k) % 4) for k in range(4)])


def tiles(v):
    rows, columns = v.shape
    return v.reshape(rows // 8, 8, columns // 128, 128).swapaxes(1, 2).reshape(-1, 128)


def untile(v, rows, columns):
    count = v.shape[0]
    v = v.reshape(count, rows // 8, columns // 128, 8, 128).swapaxes(2, 3)
    return v.reshape(count, rows, columns)


def by_offset(stack, index):
    return jnp.stack([pick(stack, (index - j) % 4) for j in range(4)])


def join_cores(mine, other, core):
    zero = jnp.where(core == 0, mine, other)
    one = jnp.where(core == 0, other, mine)
    return jnp.stack([zero, one.swapaxes(0, 1)], axis=2)


def split_cores(terms, core):
    zero = terms[:, :, 0].swapaxes(0, 1)
    one = terms[:, :, 1]
    return jnp.where(core == 0, zero, one), jnp.where(core == 0, one, zero)


def split_ahead(terms, y, x, core):
    zero = ahead(ahead(terms[:, :, 0], y).swapaxes(0, 1), x)
    one = ahead(ahead(terms[:, :, 1], y).swapaxes(0, 1), x).swapaxes(0, 1)
    return jnp.where(core == 0, zero, one), jnp.where(core == 0, one, zero)


def join_ranks(v, other, z, bit):
    low = (z & bit) == 0
    return jnp.concatenate([jnp.where(low, v, other), jnp.where(low, other, v)], axis=0)


def local(
    input_token_rows,
    output_gradient_rows,
    frozen_base_matrix,
    left_lowrank_factor,
    left_first_moment,
    left_second_moment,
    right_lowrank_factor,
    right_first_moment,
    right_second_moment,
):
    hidden_scale = 1.0 / math.sqrt(HIDDEN_UNITS)
    rank_scale = 1.0 / math.sqrt(FACTOR_RANK)
    y, x, core, z = (lax.axis_index(n) for n in ("y", "x", "core", "z"))
    p = jnp.where(core == 0, x, y)
    q = jnp.where(core == 0, y, x)

    b_block = lax.dynamic_slice_in_dim(right_lowrank_factor, (z % 2) * 128, 128, 1)
    block = jnp.concatenate([tiles(left_lowrank_factor), b_block], axis=0).astype(bf16)
    with jax.named_scope("factors_p"):
        stack = jnp.stack([block] + [shift_p(block, k) for k in (1, 2, 3)])
        a_stack = by_offset(stack[:, :224], p)
        b_stack = by_offset(stack[:, 224:], p)
        tokens, grads, base = input_token_rows, output_gradient_rows, frozen_base_matrix
        a_stack, b_stack = lax.optimization_barrier((a_stack, b_stack))
    with jax.named_scope("a_q"):
        a_stack = jnp.stack([a_stack] + [shift_q(a_stack, k) for k in (1, 2, 3)])
    a_stack, b_stack = lax.optimization_barrier((a_stack, b_stack))
    with jax.named_scope("a_cores"):
        a_stack = by_offset(a_stack, q)
        a_other = swap_core(a_stack)
    with jax.named_scope("b_q"):
        b_stack = jnp.stack([b_stack] + [shift_q(b_stack, k) for k in (1, 2, 3)])
    with jax.named_scope("act_terms"):
        a_rows = join_cores(a_stack, a_other, core).reshape(32, 224, 128)
        a_rows = untile(a_rows, 8, 3584).reshape(256, 3584)
        act_part = lax.dot_general(
            a_rows, tokens, (((1,), (1,)), ((), ())), preferred_element_type=f32
        ).reshape(4, 2, 32, 512)
        act_send = lax.dynamic_index_in_dim(act_part, 1 - z % 2, 1, keepdims=False)
        act_keep = lax.dynamic_index_in_dim(act_part, z % 2, 1, keepdims=False)
    with jax.named_scope("act_pairs"):
        act_got = flip(act_send, "z", 8, 1)
    act_got, b_stack = lax.optimization_barrier((act_got, b_stack))
    with jax.named_scope("act_shifts"):
        act_pair = act_keep + act_got
        act_pieces = [pick(act_pair, (z // 2 + k) % 4) for k in range(4)]
        act_gots = [shift_z(act_pieces[k], 2 * k) for k in range(1, 4)]
    with jax.named_scope("b_cores"):
        b_stack = by_offset(b_stack, q)
        b_rows = join_cores(b_stack, swap_core(b_stack), core).reshape(8192, 128)
    with jax.named_scope("back"):
        back_part = (
            jnp.dot(grads, b_rows, preferred_element_type=f32) * rank_scale
        ).astype(bf16).T
    back_part, act_gots = lax.optimization_barrier((back_part, act_gots))
    with jax.named_scope("back_pairs"):
        back = join_ranks(back_part, swap_pairs(back_part), z, 1)
        keep_rows, send_rows = split_ahead(back.reshape(4, 4, 2, 8, 512), y, x, core)
    with jax.named_scope("grad_b_terms"):
        act = act_pieces[0] + act_gots[0] + act_gots[1] + act_gots[2]
        act = lax.optimization_barrier((act * hidden_scale).astype(bf16))
        b_term = jnp.dot(act, grads, preferred_element_type=f32)
    keep_rows, send_rows, b_term = lax.optimization_barrier((keep_rows, send_rows, b_term))
    with jax.named_scope("grad_a_cores"):
        a_send = jnp.dot(
            send_rows.reshape(128, 512), tokens, preferred_element_type=f32
        )
        a_got = swap_core(a_send)
    with jax.named_scope("grad_a_terms"):
        a_keep = jnp.dot(
            keep_rows.reshape(128, 512), tokens, preferred_element_type=f32
        )
        a_keep = lax.optimization_barrier(a_keep)
    with jax.named_scope("grad_b_split"):
        b_term = b_term.reshape(4, 8, 4, 4, 2, 2, 128).transpose(2, 3, 4, 0, 5, 1, 6)
        b_keep, b_send = split_cores(b_term.reshape(4, 4, 2, 64, 128), core)
    with jax.named_scope("grad_b_cores"):
        b_got = swap_core(b_send)
    parts = []
    for k in range(4):
        a_part = a_keep[32 * k : 32 * k + 32] + a_got[32 * k : 32 * k + 32]
        a_part = a_part.reshape(4, 8, 28, 128).swapaxes(1, 2).reshape(4, 224, 128)
        b_part = ahead(pick(b_keep, (p + k) % 4) + pick(b_got, (p + k) % 4), q)
        parts.append(jnp.concatenate([a_part, b_part], axis=1))
    with jax.named_scope("grads_p"):
        total = parts[0]
        for k in (1, 2, 3):
            total = total + shift_p(parts[k], k)
    with jax.named_scope("grads_q"):
        parts = [total[k] for k in range(4)]
        total = parts[0]
        for k in (1, 2, 3):
            total = total + shift_q(parts[k], k)
    grad_a = total[:224] * hidden_scale
    grad_b = total[224:] * rank_scale

    squares = jnp.sum(grad_a * grad_a, axis=0) + jnp.sum(grad_b * grad_b, axis=0)
    squares = lax.all_to_all(
        jnp.broadcast_to(squares, (256, 128)), ("y", "x", "core", "z"), 0, 0, tiled=True
    )
    pair = flip(grad_b, "z", 8, 4)
    right_t = (right_lowrank_factor.T, right_first_moment.T, right_second_moment.T)
    squares, pair, right_t = lax.optimization_barrier((squares, pair, right_t))
    pair = join_ranks(grad_b, pair, z, 4)
    squares = jnp.sum(squares, keepdims=True)
    clipper = jnp.minimum(1.0, clip_limit / (jnp.sqrt(squares) + norm_epsilon))

    new_a = moment_update_step(
        tiles(left_lowrank_factor),
        tiles(left_first_moment),
        tiles(left_second_moment),
        clipper * grad_a,
    ).astype(bf16)
    copies = jnp.broadcast_to(new_a, (16, 224, 128))
    copies, pair = lax.optimization_barrier((copies, pair))
    mine = lax.all_to_all(copies, ("y", "x"), 0, 0, tiled=True)
    pairs = [pair, shift_z(pair, 1), shift_z(pair, 2), shift_z(pair, -1)]
    mine, pairs = lax.optimization_barrier((mine, pairs))
    other = swap_core(mine)
    whole_grad_b = by_offset(jnp.stack(pairs), z % 4).reshape(4, 2, 64, 128).swapaxes(0, 1)
    whole_grad_b = untile(whole_grad_b.reshape(8, 64, 128), 32, 256).reshape(256, 256)
    new_b = moment_update_step(
        *right_t, clipper * whole_grad_b
    ).astype(bf16)
    fresh = jnp.stack([jnp.where(core == 0, mine, other), jnp.where(core == 0, other, mine)], axis=1)
    new_a = untile(fresh.reshape(32, 224, 128), 8, 3584).reshape(256, 3584)
    product = lax.dot_general(new_b, new_a, (((0,), (0,)), ((), ())), preferred_element_type=f32)
    return (base.astype(f32) + product * rank_scale).astype(bf16)


def solution(mesh):
    grid = Mesh(np.asarray(mesh.devices).reshape(4, 4, 2, 8), ("y", "x", "core", "z"))
    split = P(DP, "z")
    rows = P(DP, None)
    return jax.shard_map(
        local,
        mesh=grid,
        in_specs=(split, rows, split, split, split, split, rows, rows, rows),
        out_specs=split,
        check_vma=False,
    )
```

```python
import math

import jax
import jax.numpy as jnp
import numpy as np
from jax import lax
from jax.sharding import Mesh
from jax.sharding import PartitionSpec as P

HIDDEN_UNITS = 28672
FACTOR_RANK = 256
STEP = 5000

first_decay = 0.9
second_decay = 0.999
adam_epsilon = 1e-08
learn_rate = 0.05
clip_limit = 1.0
norm_epsilon = 1e-06

bf16 = jnp.bfloat16
f32 = jnp.float32
DP = ("y", "x", "core")


def moment_update_step(param, first, second, grad):
    first_new = first_decay * first + (1.0 - first_decay) * grad
    second_new = second_decay * second + (1.0 - second_decay) * grad * grad
    first_fix = 1.0 - first_decay**STEP
    second_fix = 1.0 - second_decay**STEP
    return param - learn_rate * (first_new / first_fix) / (
        jnp.sqrt(second_new / second_fix) + adam_epsilon
    )


def dp_index(y, x, c):
    return (y * 4 + x) * 2 + c


def plane_pairs(first, k):
    pairs = []
    for y in range(4):
        for x in range(4):
            for c in range(2):
                if (c == 0) == first:
                    target = dp_index(y, (x + k) % 4, c)
                else:
                    target = dp_index((y + k) % 4, x, c)
                pairs.append((dp_index(y, x, c), target))
    return pairs


def shift_p(v, k):
    return lax.ppermute(v, DP, plane_pairs(True, k))


def shift_q(v, k):
    return lax.ppermute(v, DP, plane_pairs(False, k))


def swap_core(v):
    return lax.ppermute(v, "core", [(0, 1), (1, 0)])


def shift_z(v, k):
    return lax.ppermute(v, "z", [(i, (i + k) % 8) for i in range(8)])


def flip(v, axis, n, bit):
    return lax.ppermute(v, axis, [(i, i ^ bit) for i in range(n)])


def swap_pairs(v):
    return lax.ppermute(v, "z", [(i, (i + 1) % 8 if i % 2 else (i - 1) % 8) for i in range(8)])


def pick(stack, index):
    return lax.dynamic_index_in_dim(stack, index, 0, keepdims=False)


def ahead(stack, index):
    return jnp.stack([pick(stack, (index + k) % 4) for k in range(4)])


def tiles(v):
    rows, columns = v.shape
    return v.reshape(rows // 8, 8, columns // 128, 128).swapaxes(1, 2).reshape(-1, 128)


def untile(v, rows, columns):
    count = v.shape[0]
    v = v.reshape(count, rows // 8, columns // 128, 8, 128).swapaxes(2, 3)
    return v.reshape(count, rows, columns)


def by_offset(stack, index):
    return jnp.stack([pick(stack, (index - j) % 4) for j in range(4)])


def join_cores(mine, other, core):
    zero = jnp.where(core == 0, mine, other)
    one = jnp.where(core == 0, other, mine)
    return jnp.stack([zero, one.swapaxes(0, 1)], axis=2)


def split_cores(terms, core):
    zero = terms[:, :, 0].swapaxes(0, 1)
    one = terms[:, :, 1]
    return jnp.where(core == 0, zero, one), jnp.where(core == 0, one, zero)


def split_ahead(terms, y, x, core):
    zero = ahead(ahead(terms[:, :, 0], y).swapaxes(0, 1), x)
    one = ahead(ahead(terms[:, :, 1], y).swapaxes(0, 1), x).swapaxes(0, 1)
    return jnp.where(core == 0, zero, one), jnp.where(core == 0, one, zero)


def join_ranks(v, other, z, bit):
    low = (z & bit) == 0
    return jnp.concatenate([jnp.where(low, v, other), jnp.where(low, other, v)], axis=0)


def local(
    input_token_rows,
    output_gradient_rows,
    frozen_base_matrix,
    left_lowrank_factor,
    left_first_moment,
    left_second_moment,
    right_lowrank_factor,
    right_first_moment,
    right_second_moment,
):
    hidden_scale = 1.0 / math.sqrt(HIDDEN_UNITS)
    rank_scale = 1.0 / math.sqrt(FACTOR_RANK)
    y, x, core, z = (lax.axis_index(n) for n in ("y", "x", "core", "z"))
    p = jnp.where(core == 0, x, y)
    q = jnp.where(core == 0, y, x)

    b_block = lax.dynamic_slice_in_dim(right_lowrank_factor, (z % 2) * 128, 128, 1)
    block = jnp.concatenate([tiles(left_lowrank_factor), b_block], axis=0).astype(bf16)
    with jax.named_scope("factors_p"):
        stack = jnp.stack([block] + [shift_p(block, k) for k in (1, 2, 3)])
        a_stack = by_offset(stack[:, :224], p)
        b_stack = by_offset(stack[:, 224:], p)
        tokens, grads, base = input_token_rows, output_gradient_rows, frozen_base_matrix
        a_stack, b_stack = lax.optimization_barrier((a_stack, b_stack))
    with jax.named_scope("a_q"):
        a_stack = jnp.stack([a_stack] + [shift_q(a_stack, k) for k in (1, 2, 3)])
    a_stack, b_stack = lax.optimization_barrier((a_stack, b_stack))
    with jax.named_scope("a_cores"):
        a_stack = by_offset(a_stack, q)
        a_other = swap_core(a_stack)
    with jax.named_scope("b_q"):
        b_stack = jnp.stack([b_stack] + [shift_q(b_stack, k) for k in (1, 2, 3)])
    with jax.named_scope("act_terms"):
        a_rows = join_cores(a_stack, a_other, core).reshape(32, 224, 128)
        a_rows = untile(a_rows, 8, 3584).reshape(256, 3584)
        act_part = lax.dot_general(
            a_rows, tokens, (((1,), (1,)), ((), ())), preferred_element_type=f32
        ).reshape(4, 2, 32, 512)
        act_send = lax.dynamic_index_in_dim(act_part, 1 - z % 2, 1, keepdims=False)
        act_keep = lax.dynamic_index_in_dim(act_part, z % 2, 1, keepdims=False)
    with jax.named_scope("act_pairs"):
        act_got = jnp.concatenate(
            [flip(act_send[..., :256], "z", 8, 1), swap_pairs(act_send[..., 256:])], axis=2
        )
    act_got, b_stack = lax.optimization_barrier((act_got, b_stack))
    with jax.named_scope("act_shifts"):
        act_pair = act_keep + act_got
        act_pieces = [pick(act_pair, (z // 2 + k) % 4) for k in range(4)]
        act_gots = [shift_z(act_pieces[k], 2 * k) for k in range(1, 4)]
    with jax.named_scope("b_cores"):
        b_stack = by_offset(b_stack, q)
        b_rows = join_cores(b_stack, swap_core(b_stack), core).reshape(8192, 128)
    with jax.named_scope("back"):
        back_part = (
            jnp.dot(grads, b_rows, preferred_element_type=f32) * rank_scale
        ).astype(bf16).T
    back_part, act_gots = lax.optimization_barrier((back_part, act_gots))
    with jax.named_scope("back_pairs"):
        back = join_ranks(back_part, swap_pairs(back_part), z, 1)
        keep_rows, send_rows = split_ahead(back.reshape(4, 4, 2, 8, 512), y, x, core)
    with jax.named_scope("grad_b_terms"):
        act = act_pieces[0] + act_gots[0] + act_gots[1] + act_gots[2]
        act = lax.optimization_barrier((act * hidden_scale).astype(bf16))
        b_term = jnp.dot(act, grads, preferred_element_type=f32)
    keep_rows, send_rows, b_term = lax.optimization_barrier((keep_rows, send_rows, b_term))
    with jax.named_scope("grad_a_cores"):
        a_send = jnp.dot(
            send_rows.reshape(128, 512), tokens, preferred_element_type=f32
        )
        a_got = swap_core(a_send)
    with jax.named_scope("grad_a_terms"):
        a_keep = jnp.dot(
            keep_rows.reshape(128, 512), tokens, preferred_element_type=f32
        )
        a_keep = lax.optimization_barrier(a_keep)
    with jax.named_scope("grad_b_split"):
        b_term = b_term.reshape(4, 8, 4, 4, 2, 2, 128).transpose(2, 3, 4, 0, 5, 1, 6)
        b_keep, b_send = split_cores(b_term.reshape(4, 4, 2, 64, 128), core)
    with jax.named_scope("grad_b_cores"):
        b_got = swap_core(b_send)
    parts = []
    for k in range(4):
        a_part = a_keep[32 * k : 32 * k + 32] + a_got[32 * k : 32 * k + 32]
        a_part = a_part.reshape(4, 8, 28, 128).swapaxes(1, 2).reshape(4, 224, 128)
        b_part = ahead(pick(b_keep, (p + k) % 4) + pick(b_got, (p + k) % 4), q)
        parts.append(jnp.concatenate([a_part, b_part], axis=1))
    with jax.named_scope("grads_p"):
        total = parts[0]
        for k in (1, 2, 3):
            total = total + shift_p(parts[k], k)
    with jax.named_scope("grads_q"):
        parts = [total[k] for k in range(4)]
        total = parts[0]
        for k in (1, 2, 3):
            total = total + shift_q(parts[k], k)
    grad_a = total[:224] * hidden_scale
    grad_b = total[224:] * rank_scale

    squares = jnp.sum(grad_a * grad_a, axis=0) + jnp.sum(grad_b * grad_b, axis=0)
    squares = jnp.broadcast_to(squares, (128, 128))
    squares = squares + jnp.broadcast_to(swap_core(squares[:8])[:1], (128, 128))
    squares = lax.all_to_all(squares, ("y", "x", "z"), 0, 0, tiled=True)
    pair = flip(grad_b, "z", 8, 4)
    right_t = (right_lowrank_factor.T, right_first_moment.T, right_second_moment.T)
    squares, pair, right_t = lax.optimization_barrier((squares, pair, right_t))
    pair = join_ranks(grad_b, pair, z, 4)
    squares = jnp.sum(squares, keepdims=True)
    clipper = jnp.minimum(1.0, clip_limit / (jnp.sqrt(squares) + norm_epsilon))

    new_a = moment_update_step(
        tiles(left_lowrank_factor),
        tiles(left_first_moment),
        tiles(left_second_moment),
        clipper * grad_a,
    ).astype(bf16)
    copies = jnp.broadcast_to(new_a, (16, 224, 128))
    copies, pair = lax.optimization_barrier((copies, pair))
    mine = lax.all_to_all(copies, ("y", "x"), 0, 0, tiled=True)
    pairs = [pair, shift_z(pair, 1), shift_z(pair, 2), shift_z(pair, -1)]
    mine, pairs = lax.optimization_barrier((mine, pairs))
    other = swap_core(mine)
    whole_grad_b = by_offset(jnp.stack(pairs), z % 4).reshape(4, 2, 64, 128).swapaxes(0, 1)
    whole_grad_b = untile(whole_grad_b.reshape(8, 64, 128), 32, 256).reshape(256, 256)
    new_b = moment_update_step(
        *right_t, clipper * whole_grad_b
    ).astype(bf16)
    fresh = jnp.stack([jnp.where(core == 0, mine, other), jnp.where(core == 0, other, mine)], axis=1)
    new_a = untile(fresh.reshape(32, 224, 128), 8, 3584).reshape(256, 3584)
    product = lax.dot_general(new_b, new_a, (((0,), (0,)), ((), ())), preferred_element_type=f32)
    return (base.astype(f32) + product * rank_scale).astype(bf16)


def solution(mesh):
    grid = Mesh(np.asarray(mesh.devices).reshape(4, 4, 2, 8), ("y", "x", "core", "z"))
    split = P(DP, "z")
    rows = P(DP, None)
    return jax.shard_map(
        local,
        mesh=grid,
        in_specs=(split, rows, split, split, split, split, rows, rows, rows),
        out_specs=split,
        check_vma=False,
    )
```

```python
import math

import jax
import jax.numpy as jnp
import numpy as np
from jax import lax
from jax.sharding import Mesh
from jax.sharding import PartitionSpec as P

HIDDEN_UNITS = 28672
FACTOR_RANK = 256
STEP = 5000

first_decay = 0.9
second_decay = 0.999
adam_epsilon = 1e-08
learn_rate = 0.05
clip_limit = 1.0
norm_epsilon = 1e-06

bf16 = jnp.bfloat16
f32 = jnp.float32
DP = ("y", "x", "core")


def moment_update_step(param, first, second, grad):
    first_new = first_decay * first + (1.0 - first_decay) * grad
    second_new = second_decay * second + (1.0 - second_decay) * grad * grad
    first_fix = 1.0 - first_decay**STEP
    second_fix = 1.0 - second_decay**STEP
    return param - learn_rate * (first_new / first_fix) / (
        jnp.sqrt(second_new / second_fix) + adam_epsilon
    )


def dp_index(y, x, c):
    return (y * 4 + x) * 2 + c


def plane_pairs(first, k):
    pairs = []
    for y in range(4):
        for x in range(4):
            for c in range(2):
                if (c == 0) == first:
                    target = dp_index(y, (x + k) % 4, c)
                else:
                    target = dp_index((y + k) % 4, x, c)
                pairs.append((dp_index(y, x, c), target))
    return pairs


def shift_p(v, k):
    return lax.ppermute(v, DP, plane_pairs(True, k))


def shift_q(v, k):
    return lax.ppermute(v, DP, plane_pairs(False, k))


def shifts(shift, v):
    one, three, two = (shift(v, k) for k in (1, 3, 2))
    return jnp.stack([v, one, two, three])


def swap_core(v):
    return lax.ppermute(v, "core", [(0, 1), (1, 0)])


def shift_z(v, k):
    return lax.ppermute(v, "z", [(i, (i + k) % 8) for i in range(8)])


def flip(v, axis, n, bit):
    return lax.ppermute(v, axis, [(i, i ^ bit) for i in range(n)])


def swap_pairs(v):
    return lax.ppermute(v, "z", [(i, (i + 1) % 8 if i % 2 else (i - 1) % 8) for i in range(8)])


def pick(stack, index):
    return lax.dynamic_index_in_dim(stack, index, 0, keepdims=False)


def ahead(stack, index):
    return jnp.stack([pick(stack, (index + k) % 4) for k in range(4)])


def tiles(v):
    rows, columns = v.shape
    return v.reshape(rows // 8, 8, columns // 128, 128).swapaxes(1, 2).reshape(-1, 128)


def untile(v, rows, columns):
    count = v.shape[0]
    v = v.reshape(count, rows // 8, columns // 128, 8, 128).swapaxes(2, 3)
    return v.reshape(count, rows, columns)


def by_offset(stack, index):
    return jnp.stack([pick(stack, (index - j) % 4) for j in range(4)])


def join_cores(mine, other, core):
    zero = jnp.where(core == 0, mine, other)
    one = jnp.where(core == 0, other, mine)
    return jnp.stack([zero, one.swapaxes(0, 1)], axis=2)


def split_cores(terms, core):
    zero = terms[:, :, 0].swapaxes(0, 1)
    one = terms[:, :, 1]
    return jnp.where(core == 0, zero, one), jnp.where(core == 0, one, zero)


def split_ahead(terms, y, x, core):
    zero = ahead(ahead(terms[:, :, 0], y).swapaxes(0, 1), x)
    one = ahead(ahead(terms[:, :, 1], y).swapaxes(0, 1), x).swapaxes(0, 1)
    return jnp.where(core == 0, zero, one), jnp.where(core == 0, one, zero)


def join_ranks(v, other, z, bit):
    low = (z & bit) == 0
    return jnp.concatenate([jnp.where(low, v, other), jnp.where(low, other, v)], axis=0)


def local(
    input_token_rows,
    output_gradient_rows,
    frozen_base_matrix,
    left_lowrank_factor,
    left_first_moment,
    left_second_moment,
    right_lowrank_factor,
    right_first_moment,
    right_second_moment,
):
    hidden_scale = 1.0 / math.sqrt(HIDDEN_UNITS)
    rank_scale = 1.0 / math.sqrt(FACTOR_RANK)
    y, x, core, z = (lax.axis_index(n) for n in ("y", "x", "core", "z"))
    p = jnp.where(core == 0, x, y)
    q = jnp.where(core == 0, y, x)

    b_block = lax.dynamic_slice_in_dim(right_lowrank_factor, (z % 2) * 128, 128, 1)
    block = jnp.concatenate([tiles(left_lowrank_factor), b_block], axis=0).astype(bf16)
    with jax.named_scope("factors_p"):
        stack = shifts(shift_p, block)
        a_stack = by_offset(stack[:, :224], p)
        b_stack = by_offset(stack[:, 224:], p)
        tokens, grads, base = input_token_rows, output_gradient_rows, frozen_base_matrix
        a_stack, b_stack = lax.optimization_barrier((a_stack, b_stack))
    with jax.named_scope("a_q"):
        a_stack = shifts(shift_q, a_stack)
    a_stack, b_stack = lax.optimization_barrier((a_stack, b_stack))
    with jax.named_scope("a_cores"):
        a_stack = by_offset(a_stack, q)
        a_other = swap_core(a_stack)
    with jax.named_scope("b_q"):
        b_stack = shifts(shift_q, b_stack)
    with jax.named_scope("act_terms"):
        a_rows = join_cores(a_stack, a_other, core).reshape(32, 224, 128)
        a_rows = untile(a_rows, 8, 3584).reshape(256, 3584)
        act_part = lax.dot_general(
            a_rows, tokens, (((1,), (1,)), ((), ())), preferred_element_type=f32
        ).reshape(4, 2, 32, 512)
        act_send = lax.dynamic_index_in_dim(act_part, 1 - z % 2, 1, keepdims=False)
        act_keep = lax.dynamic_index_in_dim(act_part, z % 2, 1, keepdims=False)
    with jax.named_scope("act_pairs"):
        act_got = jnp.concatenate(
            [flip(act_send[..., :256], "z", 8, 1), swap_pairs(act_send[..., 256:])], axis=2
        )
    act_got, b_stack = lax.optimization_barrier((act_got, b_stack))
    with jax.named_scope("act_shifts"):
        act_pair = act_keep + act_got
        act_pieces = [pick(act_pair, (z // 2 + k) % 4) for k in range(4)]
        act_gots = [shift_z(act_pieces[k], 2 * k) for k in range(1, 4)]
    with jax.named_scope("b_cores"):
        b_stack = by_offset(b_stack, q)
        b_rows = join_cores(b_stack, swap_core(b_stack), core).reshape(8192, 128)
    with jax.named_scope("back"):
        back_part = (
            jnp.dot(grads, b_rows, preferred_element_type=f32) * rank_scale
        ).astype(bf16).T
    back_part, act_gots = lax.optimization_barrier((back_part, act_gots))
    with jax.named_scope("back_pairs"):
        back = join_ranks(back_part, swap_pairs(back_part), z, 1)
        keep_rows, send_rows = split_ahead(back.reshape(4, 4, 2, 8, 512), y, x, core)
    with jax.named_scope("grad_b_terms"):
        act = act_pieces[0] + act_gots[0] + act_gots[1] + act_gots[2]
        act = lax.optimization_barrier((act * hidden_scale).astype(bf16))
        b_term = jnp.dot(act, grads, preferred_element_type=f32)
    keep_rows, send_rows, b_term = lax.optimization_barrier((keep_rows, send_rows, b_term))
    with jax.named_scope("grad_a_cores"):
        a_send = jnp.dot(
            send_rows.reshape(128, 512), tokens, preferred_element_type=f32
        )
        a_got = swap_core(a_send)
    with jax.named_scope("grad_a_terms"):
        a_keep = jnp.dot(
            keep_rows.reshape(128, 512), tokens, preferred_element_type=f32
        )
        a_keep = lax.optimization_barrier(a_keep)
    with jax.named_scope("grad_b_split"):
        b_term = b_term.reshape(4, 8, 4, 4, 2, 2, 128).transpose(2, 3, 4, 0, 5, 1, 6)
        b_keep, b_send = split_cores(b_term.reshape(4, 4, 2, 64, 128), core)
    with jax.named_scope("grad_b_cores"):
        b_got = swap_core(b_send)
    parts = []
    for k in range(4):
        a_part = a_keep[32 * k : 32 * k + 32] + a_got[32 * k : 32 * k + 32]
        a_part = a_part.reshape(4, 8, 28, 128).swapaxes(1, 2).reshape(4, 224, 128)
        b_part = ahead(pick(b_keep, (p + k) % 4) + pick(b_got, (p + k) % 4), q)
        parts.append(jnp.concatenate([a_part, b_part], axis=1))
    with jax.named_scope("grads_p"):
        total = parts[0]
        for k in (1, 3, 2):
            total = total + shift_p(parts[k], k)
    with jax.named_scope("grads_q"):
        parts = [total[k] for k in range(4)]
        total = parts[0]
        for k in (1, 3, 2):
            total = total + shift_q(parts[k], k)
    grad_a = total[:224] * hidden_scale
    grad_b = total[224:] * rank_scale

    squares = jnp.sum(grad_a * grad_a, axis=0) + jnp.sum(grad_b * grad_b, axis=0)
    squares = jnp.broadcast_to(squares, (128, 128))
    squares = squares + jnp.broadcast_to(swap_core(squares[:8])[:1], (128, 128))
    squares = lax.all_to_all(squares, ("y", "x", "z"), 0, 0, tiled=True)
    pair = flip(grad_b, "z", 8, 1)
    right_t = (right_lowrank_factor.T, right_first_moment.T, right_second_moment.T)
    squares, pair, right_t = lax.optimization_barrier((squares, pair, right_t))
    pair = join_ranks(grad_b, pair, z, 1)
    squares = jnp.sum(squares, keepdims=True)
    clipper = jnp.minimum(1.0, clip_limit / (jnp.sqrt(squares) + norm_epsilon))

    new_a = moment_update_step(
        tiles(left_lowrank_factor),
        tiles(left_first_moment),
        tiles(left_second_moment),
        clipper * grad_a,
    ).astype(bf16)
    copies = jnp.broadcast_to(new_a, (16, 224, 128))
    copies, pair = lax.optimization_barrier((copies, pair))
    mine = lax.all_to_all(copies, ("y", "x"), 0, 0, tiled=True)
    pairs = [pair] + [shift_z(pair, 2 * k) for k in (1, 2, 3)]
    mine, pairs = lax.optimization_barrier((mine, pairs))
    other = swap_core(mine)
    whole_grad_b = by_offset(jnp.stack(pairs), z // 2).reshape(8, 64, 128)
    whole_grad_b = untile(whole_grad_b, 32, 256).reshape(256, 256)
    new_b = moment_update_step(
        *right_t, clipper * whole_grad_b
    ).astype(bf16)
    fresh = jnp.stack([jnp.where(core == 0, mine, other), jnp.where(core == 0, other, mine)], axis=1)
    new_a = untile(fresh.reshape(32, 224, 128), 8, 3584).reshape(256, 3584)
    product = lax.dot_general(new_b, new_a, (((0,), (0,)), ((), ())), preferred_element_type=f32)
    return (base.astype(f32) + product * rank_scale).astype(bf16)


def solution(mesh):
    grid = Mesh(np.asarray(mesh.devices).reshape(4, 4, 2, 8), ("y", "x", "core", "z"))
    split = P(DP, "z")
    rows = P(DP, None)
    return jax.shard_map(
        local,
        mesh=grid,
        in_specs=(split, rows, split, split, split, split, rows, rows, rows),
        out_specs=split,
        check_vma=False,
    )
```

```python
import math

import jax
import jax.numpy as jnp
import numpy as np
from jax import lax
from jax.sharding import Mesh
from jax.sharding import PartitionSpec as P

HIDDEN_UNITS = 28672
FACTOR_RANK = 256
STEP = 5000

first_decay = 0.9
second_decay = 0.999
adam_epsilon = 1e-08
learn_rate = 0.05
clip_limit = 1.0
norm_epsilon = 1e-06

bf16 = jnp.bfloat16
f32 = jnp.float32
DP = ("y", "x", "core")


def moment_update_step(param, first, second, grad):
    first_new = first_decay * first + (1.0 - first_decay) * grad
    second_new = second_decay * second + (1.0 - second_decay) * grad * grad
    first_fix = 1.0 - first_decay**STEP
    second_fix = 1.0 - second_decay**STEP
    return param - learn_rate * (first_new / first_fix) / (
        jnp.sqrt(second_new / second_fix) + adam_epsilon
    )


def dp_index(y, x, c):
    return (y * 4 + x) * 2 + c


def plane_pairs(first, k):
    pairs = []
    for y in range(4):
        for x in range(4):
            for c in range(2):
                if (c == 0) == first:
                    target = dp_index(y, (x + k) % 4, c)
                else:
                    target = dp_index((y + k) % 4, x, c)
                pairs.append((dp_index(y, x, c), target))
    return pairs


def shift_p(v, k):
    return lax.ppermute(v, DP, plane_pairs(True, k))


def shift_q(v, k):
    return lax.ppermute(v, DP, plane_pairs(False, k))


def shifts(shift, v):
    one, three, two = (shift(v, k) for k in (1, 3, 2))
    return jnp.stack([v, one, two, three])


def swap_core(v):
    return lax.ppermute(v, "core", [(0, 1), (1, 0)])


def shift_z(v, k):
    return lax.ppermute(v, "z", [(i, (i + k) % 8) for i in range(8)])


def flip(v, axis, n, bit):
    return lax.ppermute(v, axis, [(i, i ^ bit) for i in range(n)])


def swap_pairs(v):
    return lax.ppermute(v, "z", [(i, (i + 1) % 8 if i % 2 else (i - 1) % 8) for i in range(8)])


def pick(stack, index):
    return lax.dynamic_index_in_dim(stack, index, 0, keepdims=False)


def ahead(stack, index):
    return jnp.stack([pick(stack, (index + k) % 4) for k in range(4)])


def tiles(v):
    rows, columns = v.shape
    return v.reshape(rows // 8, 8, columns // 128, 128).swapaxes(1, 2).reshape(-1, 128)


def untile(v, rows, columns):
    count = v.shape[0]
    v = v.reshape(count, rows // 8, columns // 128, 8, 128).swapaxes(2, 3)
    return v.reshape(count, rows, columns)


def by_offset(stack, index):
    return jnp.stack([pick(stack, (index - j) % 4) for j in range(4)])


def join_cores(mine, other, core):
    zero = jnp.where(core == 0, mine, other)
    one = jnp.where(core == 0, other, mine)
    return jnp.stack([zero, one.swapaxes(0, 1)], axis=2)


def split_cores(terms, core):
    zero = terms[:, :, 0].swapaxes(0, 1)
    one = terms[:, :, 1]
    return jnp.where(core == 0, zero, one), jnp.where(core == 0, one, zero)


def split_ahead(terms, y, x, core):
    zero = ahead(ahead(terms[:, :, 0], y).swapaxes(0, 1), x)
    one = ahead(ahead(terms[:, :, 1], y).swapaxes(0, 1), x).swapaxes(0, 1)
    return jnp.where(core == 0, zero, one), jnp.where(core == 0, one, zero)


def join_ranks(v, other, z, bit):
    low = (z & bit) == 0
    return jnp.concatenate([jnp.where(low, v, other), jnp.where(low, other, v)], axis=0)


def local(
    input_token_rows,
    output_gradient_rows,
    frozen_base_matrix,
    left_lowrank_factor,
    left_first_moment,
    left_second_moment,
    right_lowrank_factor,
    right_first_moment,
    right_second_moment,
):
    hidden_scale = 1.0 / math.sqrt(HIDDEN_UNITS)
    rank_scale = 1.0 / math.sqrt(FACTOR_RANK)
    y, x, core, z = (lax.axis_index(n) for n in ("y", "x", "core", "z"))
    p = jnp.where(core == 0, x, y)
    q = jnp.where(core == 0, y, x)

    b_block = lax.dynamic_slice_in_dim(right_lowrank_factor, (z % 2) * 128, 128, 1)
    block = jnp.concatenate([tiles(left_lowrank_factor), b_block], axis=0).astype(bf16)
    with jax.named_scope("factors_p"):
        stack = shifts(shift_p, block)
        a_stack = by_offset(stack[:, :224], p)
        b_stack = by_offset(stack[:, 224:], p)
        tokens, grads, base = input_token_rows, output_gradient_rows, frozen_base_matrix
        a_stack, b_stack = lax.optimization_barrier((a_stack, b_stack))
    with jax.named_scope("a_q"):
        a_stack = shifts(shift_q, a_stack)
    a_stack, b_stack = lax.optimization_barrier((a_stack, b_stack))
    with jax.named_scope("a_cores"):
        a_stack = by_offset(a_stack, q)
        a_other = swap_core(a_stack)
    with jax.named_scope("b_q"):
        b_stack = shifts(shift_q, b_stack)
    with jax.named_scope("act_terms"):
        a_rows = join_cores(a_stack, a_other, core).reshape(32, 224, 128)
        a_rows = untile(a_rows, 8, 3584).reshape(256, 3584)
        act_part = lax.dot_general(
            a_rows, tokens, (((1,), (1,)), ((), ())), preferred_element_type=f32
        ).reshape(4, 2, 32, 512)
        act_send = lax.dynamic_index_in_dim(act_part, 1 - z % 2, 1, keepdims=False)
        act_keep = lax.dynamic_index_in_dim(act_part, z % 2, 1, keepdims=False)
    with jax.named_scope("act_pairs"):
        act_got = jnp.concatenate(
            [flip(act_send[..., :256], "z", 8, 1), swap_pairs(act_send[..., 256:])], axis=2
        )
    act_got, b_stack = lax.optimization_barrier((act_got, b_stack))
    with jax.named_scope("act_shifts"):
        act_pair = act_keep + act_got
        act_pieces = [pick(act_pair, (z // 2 + k) % 4) for k in range(4)]
        act_gots = [shift_z(act_pieces[k], 2 * k) for k in (1, 3, 2)]
    with jax.named_scope("b_cores"):
        b_stack = by_offset(b_stack, q)
        b_rows = join_cores(b_stack, swap_core(b_stack), core).reshape(8192, 128)
    with jax.named_scope("back"):
        back_part = (
            jnp.dot(grads, b_rows, preferred_element_type=f32) * rank_scale
        ).astype(bf16).T
    back_part, act_gots = lax.optimization_barrier((back_part, act_gots))
    with jax.named_scope("back_pairs"):
        back = join_ranks(back_part, swap_pairs(back_part), z, 1)
        keep_rows, send_rows = split_ahead(back.reshape(4, 4, 2, 8, 512), y, x, core)
    with jax.named_scope("grad_b_terms"):
        act = act_pieces[0] + act_gots[0] + act_gots[1] + act_gots[2]
        act = lax.optimization_barrier((act * hidden_scale).astype(bf16))
        b_term = jnp.dot(act, grads, preferred_element_type=f32)
    keep_rows, send_rows, b_term = lax.optimization_barrier((keep_rows, send_rows, b_term))
    with jax.named_scope("grad_a_cores"):
        a_send = jnp.dot(
            send_rows.reshape(128, 512), tokens, preferred_element_type=f32
        )
        a_got = swap_core(a_send)
    with jax.named_scope("grad_a_terms"):
        a_keep = jnp.dot(
            keep_rows.reshape(128, 512), tokens, preferred_element_type=f32
        )
        a_keep = lax.optimization_barrier(a_keep)
    with jax.named_scope("grad_b_split"):
        b_term = b_term.reshape(4, 8, 4, 4, 2, 2, 128).transpose(2, 3, 4, 0, 5, 1, 6)
        b_keep, b_send = split_cores(b_term.reshape(4, 4, 2, 64, 128), core)
    with jax.named_scope("grad_b_cores"):
        b_got = swap_core(b_send)
    parts = []
    for k in range(4):
        a_part = a_keep[32 * k : 32 * k + 32] + a_got[32 * k : 32 * k + 32]
        a_part = a_part.reshape(4, 8, 28, 128).swapaxes(1, 2).reshape(4, 224, 128)
        b_part = ahead(pick(b_keep, (p + k) % 4) + pick(b_got, (p + k) % 4), q)
        parts.append(jnp.concatenate([a_part, b_part], axis=1))
    with jax.named_scope("grads_p"):
        total = parts[0]
        for k in (1, 3, 2):
            total = total + shift_p(parts[k], k)
    with jax.named_scope("grads_q"):
        parts = [total[k] for k in range(4)]
        total = parts[0]
        for k in (1, 3, 2):
            total = total + shift_q(parts[k], k)
    grad_a = total[:224] * hidden_scale
    grad_b = total[224:] * rank_scale

    squares = jnp.sum(grad_a * grad_a, axis=0) + jnp.sum(grad_b * grad_b, axis=0)
    squares = jnp.broadcast_to(squares, (128, 128))
    squares = squares + jnp.broadcast_to(swap_core(squares[:8])[:1], (128, 128))
    squares = lax.all_to_all(squares, ("y", "x", "z"), 0, 0, tiled=True)
    pair = flip(grad_b, "z", 8, 1)
    right_t = (right_lowrank_factor.T, right_first_moment.T, right_second_moment.T)
    squares, pair, right_t = lax.optimization_barrier((squares, pair, right_t))
    pair = join_ranks(grad_b, pair, z, 1)
    squares = jnp.sum(squares, keepdims=True)
    clipper = jnp.minimum(1.0, clip_limit / (jnp.sqrt(squares) + norm_epsilon))

    new_a = moment_update_step(
        tiles(left_lowrank_factor),
        tiles(left_first_moment),
        tiles(left_second_moment),
        clipper * grad_a,
    ).astype(bf16)
    copies = jnp.broadcast_to(new_a, (16, 224, 128))
    copies, pair = lax.optimization_barrier((copies, pair))
    mine = lax.all_to_all(copies, ("y", "x"), 0, 0, tiled=True)
    pairs = shifts(lambda v, k: shift_z(v, 2 * k), pair)
    mine, pairs = lax.optimization_barrier((mine, pairs))
    other = swap_core(mine)
    whole_grad_b = by_offset(pairs, z // 2).reshape(8, 64, 128)
    whole_grad_b = untile(whole_grad_b, 32, 256).reshape(256, 256)
    new_b = moment_update_step(
        *right_t, clipper * whole_grad_b
    ).astype(bf16)
    fresh = jnp.stack([jnp.where(core == 0, mine, other), jnp.where(core == 0, other, mine)], axis=1)
    new_a = untile(fresh.reshape(32, 224, 128), 8, 3584).reshape(256, 3584)
    product = lax.dot_general(new_b, new_a, (((0,), (0,)), ((), ())), preferred_element_type=f32)
    return (base.astype(f32) + product * rank_scale).astype(bf16)


def solution(mesh):
    grid = Mesh(np.asarray(mesh.devices).reshape(4, 4, 2, 8), ("y", "x", "core", "z"))
    split = P(DP, "z")
    rows = P(DP, None)
    return jax.shard_map(
        local,
        mesh=grid,
        in_specs=(split, rows, split, split, split, split, rows, rows, rows),
        out_specs=split,
        check_vma=False,
    )
```
